32 devices in a mesh: blk: 8 (over z, y), lblk: 4 (over x, core).
Axes of the slice: x: 2, y: 2, z: 4, core: 2. Of those that a mesh axis runs over, the one named last changes fastest.
Arguments:
- partial_rows: bfloat16 [4, 8192, 1024], P('lblk', 'blk'), may hold values from -5 to 5
- row_owner: int32 [4, 8192, 1], P('lblk', 'blk'), may hold values from 0 to 7; in each aligned block of 1024 rows (0 to 1023, 1024 to 2047, ..., all dimensions but the last counted through in order) at most 128 rows name the same one
- row_key: int32 [4, 8192], P('lblk', 'blk'), may hold values from 0 to 127
- azimuth_orders: int32 [8], replicated, may hold values from 1 to 4095, as said below
- legendre_table: bfloat16 [8, 4096, 256], P('blk', 'lblk'), may hold values from -0.375 to 0.375
- spin_even: bfloat16 [8, 4096, 256], P('blk', 'lblk'), may hold values from -0.375 to 0.375
- spin_odd: bfloat16 [8, 4096, 256], P('blk', 'lblk'), may hold values from -0.375 to 0.375
Outputs:
- eigenvalues: float32 [2, 2, 4, 64, 8192], P(None, None, 'lblk', 'blk')
- cycle_maps: float32 [2, 4, 64, 8192], P(None, 'lblk', 'blk')
The draws below stay inside these ranges and needn't reach their ends.
Inputs may be any that keep to these rules, and one draw needn't show every extreme that they name: `row_owner`: no more than 128 rows of one device name the same owner; some device sends exactly 128 rows to some owner in every draw. `azimuth_orders`: all distinct; 1 and 4095 are always among them.
All inputs are finite; a program needn't handle non-finite values.
Results may differ from the reference program's by a relative error of at most 0.0041.
Values may be sent and summed in bfloat16 or wider, within the bound.
A program may use at most 128 MiB of HBM per device.

```python
import math
import jax
import jax.numpy as jnp
import numpy as np
from jax import lax

NPHI = 8192
L = 4096
SEG = 1024
R_DEV = 8
PR = 1024
KEYS = 128
CAP = 128
SLICES = 4
SLICE_CYCLES = 64
CYCLES = 256
SLICE_ROWS = 8192
M = 8
N_BLK = 8


def draw_azimuth_orders(key, part):
    candidates = jax.random.permutation(jax.random.fold_in(key, 5), L - 3).astype(jnp.int32) + 2
    chosen = jnp.concatenate([candidates[:M - 2], jnp.array([1, L - 1], jnp.int32)])
    return jax.random.permutation(jax.random.fold_in(key, 9), chosen).astype(jnp.int32)


def set_ends(drawn, key, low, top_value):
    longest = drawn.shape.index(max(drawn.shape))
    spots = []
    for shift in (0, 1):
        where = [jax.random.randint(jax.random.fold_in(key, axis), (), 0, length) for axis, length in enumerate(drawn.shape)]
        where[longest] = (where[longest] + shift) % drawn.shape[longest]
        spots.append(tuple(where))
    return drawn.at[spots[0]].set(low).at[spots[1]].set(top_value)


def levels(rng, extent, pieces, smallest, top_value):
    loudness = 1.0
    for axis_at, blocks in pieces:
        heights = jax.random.uniform(jax.random.fold_in(jax.random.fold_in(rng, 6), axis_at), (blocks,), jnp.float32, smallest / len(pieces), top_value / len(pieces))
        loudness = loudness * jnp.repeat(jnp.exp(heights), extent[axis_at] // blocks).reshape((-1,) + (1,) * (len(extent) - 1 - axis_at))
    return loudness


def deal_out(stream_key, own, number, rows, number_of, top, most, lean):
    ranking = jax.random.permutation(stream_key, number_of)
    heavy_load, usual = portions_of(number_of, rows * top, most, lean, True), portions_of(number_of, rows * top, most, lean, False)
    places = jnp.arange(number_of)

    def named(sizes, offset_by):
        used = int((sizes > 0).sum())
        fixed = max(1, used // 4)
        moved = fixed + (places - fixed + offset_by * (used - fixed)) % max(1, number_of - fixed)
        return jnp.zeros((number_of,), jnp.int32).at[ranking[jnp.where(places < fixed, places, moved)]].set(jnp.asarray(sizes, jnp.int32))

    sizes = jnp.where(number % 4 == 0, named(heavy_load, number // 4), named(usual, number - number // 4 - 1))
    mixed = jax.random.permutation(jax.random.fold_in(own, 3), number_of)
    source_of, sink = mixed[0:number_of // 2 * 2:2], mixed[1:number_of // 2 * 2:2]
    margin = jnp.minimum(sizes[source_of] - 1, most - sizes[sink]) // 2
    margin = jnp.where((source_of == ranking[0]) | (sink == ranking[0]) | (sizes[sink] == 0), 0, jnp.maximum(margin, 0))
    moved = jax.random.randint(jax.random.fold_in(own, 4), (number_of // 2,), 0, 1 << 20) % (margin + 1)
    sizes = sizes.at[source_of].add(-moved).at[sink].add(moved)
    items = jnp.searchsorted(jnp.cumsum(sizes), jnp.arange(rows * top), side="right").astype(jnp.int32)
    table = items.reshape(top, rows).T
    table = table[jax.random.permutation(jax.random.fold_in(own, 1), rows)]
    offset_by = jax.random.randint(jax.random.fold_in(own, 2), (rows, 1), 0, top)
    return jnp.take_along_axis(table, (jnp.arange(top)[None, :] + offset_by) % top, axis=1)


def portions_of(amount, total, limit, lean, full):
    loads = [(1 << 20) // math.isqrt(standing ** lean) + 1 for standing in range(1, amount + 1)]
    largest = limit if full else min(limit, max(-(-total // amount), total * loads[0] // sum(loads)))
    least = 1 if total - largest >= amount - 1 else 0
    counts, rest = [largest] + [least] * (amount - 1), total - largest - least * (amount - 1)
    while rest > 0:
        free = [i for i in range(1, amount) if counts[i] < largest] or [i for i in range(1, amount) if counts[i] < limit]
        pool, remaining = sum([loads[i] for i in free]), rest
        for i in free:
            more = min(limit - counts[i], max(1, remaining * loads[i] // pool), rest)
            counts[i] = counts[i] + more
            rest = rest - more
    return np.array(counts)


def gaussian(own_key, dims, spread, most, pieces=(), dtype=jnp.bfloat16):
    entries = jax.random.normal(own_key, dims, jnp.float32) * spread
    if len(pieces) > 0:
        entries = levels(own_key, dims, pieces, -0.22, 0.18) * entries
    return jnp.clip(entries, min=-most, max=most).astype(dtype)


def setup_inputs(seed: int = 0) -> dict:
    seeds = jax.random.split(jax.random.key(seed), 8)
    partial_rows = gaussian(seeds[0], (SLICES, SLICE_ROWS, SEG), 0.35, 5.0, ((0, 4), (1, 8)))
    row_owner_keys = jax.random.split(jax.random.fold_in(seeds[1], 1), SLICES * SLICE_ROWS // PR)
    row_owner_turns = jax.random.permutation(jax.random.fold_in(seeds[1], 3), SLICES * SLICE_ROWS // PR)
    row_owner = jax.vmap(lambda own, number: deal_out(jax.random.fold_in(seeds[1], 2), own, number, PR, N_BLK, 1, CAP, 2))(row_owner_keys, row_owner_turns).reshape((SLICES, SLICE_ROWS, 1))
    row_key = set_ends(jax.random.randint(seeds[2], (SLICES, SLICE_ROWS), 0, KEYS), jax.random.fold_in(seeds[2], 1), 0, KEYS - 1).astype(jnp.int32)
    azimuth_orders = draw_azimuth_orders(jax.random.fold_in(seeds[7], 71), 0)
    legendre_table = gaussian(seeds[4], (M, L, CYCLES), CYCLES ** -0.5, 0.375, ((0, 8), (1, 4)))
    spin_even = gaussian(seeds[5], (M, L, CYCLES), CYCLES ** -0.5, 0.375, ((0, 8), (1, 4)))
    spin_odd = gaussian(seeds[6], (M, L, CYCLES), CYCLES ** -0.5, 0.375, ((0, 8), (1, 4)))
    return {"partial_rows": partial_rows, "row_owner": row_owner, "row_key": row_key, "azimuth_orders": azimuth_orders, "legendre_table": legendre_table, "spin_even": spin_even, "spin_odd": spin_odd}


def wave_table(azimuth_orders, length):
    orders = azimuth_orders.shape[0]
    phase_index = lax.broadcasted_iota(jnp.int32, (orders, length), 1) * azimuth_orders[:, None] % length
    angles = phase_index.astype(jnp.float32) * (2.0 * math.pi / length)
    return jnp.concatenate([jnp.cos(angles), jnp.sin(angles)], axis=0)

def degree_factors(degree):
    smoothing = jnp.exp(-2.0 * degree * (degree + 1.0) / (L * L))
    factor = jnp.sqrt(jnp.maximum((degree - 1.0) * (degree + 2.0), 0.0) / jnp.maximum(degree * (degree + 1.0), 1.0))
    return (smoothing, factor)

def eigen_pair(coefficients, waves):
    orders = coefficients.shape[1]
    real_part = coefficients[..., 0]
    imag_part = coefficients[..., 1]
    real_all = jnp.concatenate([real_part[:, :, :2], -imag_part[:, :, 2:]], axis=2)
    imag_all = jnp.concatenate([imag_part[:, :, :2], real_part[:, :, 2:]], axis=2)
    stacked = jnp.concatenate([real_all, -imag_all], axis=1)
    fields = lax.dot_general(stacked, waves, (((1,), (0,)), ((), ())), precision=lax.Precision.HIGHEST) * (2.0 / math.sqrt(orders))
    half_trace = 0.5 * fields[:, 0]
    shear_size = jnp.sqrt(fields[:, 1] * fields[:, 1] + fields[:, 2] * fields[:, 2])
    return jnp.stack([half_trace + shear_size, half_trace - shear_size], axis=0)

def reference(partial_rows, row_owner, row_key, azimuth_orders, legendre_table, spin_even, spin_odd):
    values = partial_rows.reshape(SLICES * SLICE_ROWS, SEG).astype(jnp.float32)
    slice_index = lax.broadcasted_iota(jnp.int32, (SLICES, SLICE_ROWS), 0)
    target = ((slice_index * N_BLK + row_owner[:, :, 0]) * KEYS + row_key).reshape(-1).astype(jnp.int32)
    blocks = jax.ops.segment_sum(values, target, num_segments=SLICES * N_BLK * KEYS)
    shell_maps = blocks.reshape(SLICES, N_BLK, 2, R_DEV, NPHI).transpose(2, 0, 1, 3, 4)
    cycle_out = shell_maps.reshape(2, SLICES, SLICE_CYCLES, NPHI)
    cycle_maps = shell_maps.reshape(2 * CYCLES, NPHI)
    waves = wave_table(azimuth_orders, NPHI)
    spectra = lax.dot_general(cycle_maps, waves, (((1,), (1,)), ((), ())), precision=lax.Precision.HIGHEST) / math.sqrt(NPHI)
    sign_flip = jnp.array([1.0, -1.0], jnp.float32).reshape(1, 1, 2, 1)
    spectra = spectra.reshape(2, CYCLES, 2, M) * sign_flip
    harmonics = spectra.transpose(3, 0, 2, 1).reshape(M, 4, CYCLES).astype(jnp.bfloat16)
    smoothing, factor = degree_factors(jnp.arange(L).astype(jnp.float32))

    def single_order(operands):
        spectrum, legendre, even_table, odd_table = operands
        coefficients = jnp.dot(legendre, spectrum.T, preferred_element_type=jnp.float32)
        trace_terms = (smoothing[:, None] * coefficients).astype(jnp.bfloat16)
        shear_terms = ((-0.5 * smoothing * factor)[:, None] * coefficients).astype(jnp.bfloat16)
        return jnp.stack([jnp.dot(legendre.T, trace_terms, preferred_element_type=jnp.float32), jnp.dot(even_table.T, shear_terms, preferred_element_type=jnp.float32), jnp.dot(odd_table.T, shear_terms, preferred_element_type=jnp.float32)], axis=1)
    synthesis = lax.map(single_order, (harmonics, legendre_table, spin_even, spin_odd)).astype(jnp.bfloat16)
    coefficients = synthesis.astype(jnp.float32).transpose(1, 0, 2, 3).reshape(CYCLES, M, 3, 2, 2)
    eigen = eigen_pair(coefficients, waves)
    return (eigen.transpose(0, 2, 1, 3).reshape(2, 2, SLICES, SLICE_CYCLES, NPHI), cycle_out)
```

```python
import functools
import math

import jax
import jax.numpy as jnp
from jax import lax
from jax.experimental import pallas as pl
from jax.experimental.pallas import tpu as pltpu
from jax.sharding import PartitionSpec as P

NPHI = 8192
SEG = 1024
R_DEV = 8
SHELLS = 2
POS = NPHI // SEG
KEYS = SHELLS * R_DEV * POS
LANES = 128
GROUP = 2 * SHELLS * R_DEV
INNER = 2
MESH = pl.DeviceIdType.MESH
F32 = jnp.float32
BF16 = jnp.bfloat16


def split(value):
    high = value.astype(BF16)
    low = (value - high.astype(F32)).astype(BF16)
    return jnp.concatenate([high, low], axis=0)


def dot_nt(a, b):
    return lax.dot_general(a, b, (((1,), (1,)), ((), ())), preferred_element_type=F32)


def iota(shape, axis):
    return lax.broadcasted_iota(jnp.int32, shape, axis)


def kernel(
    n, nl, degrees,
    rows_hbm, owner_ref, key_ref, order_ref, table_hbm, even_hbm, odd_hbm,
    eigen_ref, cycle_ref,
    rows, table, even, odd, waves, send_y, local, recv_y, send_z, recv_z,
    send1, recv1, send2, recv2,
    load_sem, y_send, y_recv, z_send, z_recv, s1_send, s1_recv, s2_send, s2_recv,
):
    total = n * nl
    depth = n // INNER
    me_b = lax.axis_index("blk")
    me_l = lax.axis_index("lblk")
    me = me_l * n + me_b
    my_z = me_b // INNER
    my_y = me_b % INNER
    pair = my_z * INNER + (INNER - 1 - my_y)

    loads = [
        pltpu.make_async_copy(src, dst, load_sem.at[at])
        for at, (src, dst) in enumerate(
            ((rows_hbm.at[0], rows), (table_hbm.at[0], table), (even_hbm.at[0], even), (odd_hbm.at[0], odd))
        )
    ]
    for load in loads:
        load.start()

    barrier = pltpu.get_barrier_semaphore()

    def greet(step, carry):
        to = lax.rem(me + step, total)
        pl.semaphore_signal(barrier, inc=1, device_id=(lax.rem(to, n), to // n), device_id_type=MESH)
        return carry

    lax.fori_loop(1, total, greet, 0)

    keys = key_ref[...]
    owners = owner_ref[...]
    slot = (keys % POS) * (SHELLS * R_DEV) + keys // POS
    orders = order_ref[...]
    m = orders.shape[0]
    phase = (iota((m, SEG), 1) * orders) % NPHI
    angle = phase.astype(F32) * (2.0 * math.pi / NPHI)
    wave_c, wave_s = jnp.cos(angle), jnp.sin(angle)

    loads[0].wait()
    pl.semaphore_wait(barrier, total - 1)

    def partial(owner):
        chosen = jnp.where(owners == owner, slot, -1)
        one_hot = jnp.where(iota((KEYS, owners.shape[1]), 0) == chosen, 1.0, 0.0).astype(BF16)
        return jnp.dot(one_hot, rows[...], preferred_element_type=F32).astype(BF16)

    def target_z(t):
        return lax.rem(my_z + 1 + t, depth)

    def y_copy(t):
        return pltpu.make_async_remote_copy(
            src_ref=send_y.at[t], dst_ref=recv_y.at[t], send_sem=y_send.at[t], recv_sem=y_recv.at[t],
            device_id=(pair, me_l), device_id_type=MESH,
        )

    def z_copy(t):
        return pltpu.make_async_remote_copy(
            src_ref=send_z.at[t], dst_ref=recv_z.at[t], send_sem=z_send.at[t], recv_sem=z_recv.at[t],
            device_id=(target_z(t) * INNER + my_y, me_l), device_id_type=MESH,
        )

    def first(t, carry):
        send_y[t] = partial(target_z(t) * INNER + (INNER - 1 - my_y))
        y_copy(t).start()
        return carry

    lax.fori_loop(0, depth, first, 0)

    spectra = dot_nt(split(jnp.concatenate([wave_c, wave_s], axis=0)), rows[...])
    spectra = spectra[: 2 * m] + spectra[2 * m :]
    turn = ((orders * (keys % POS)) % POS).astype(F32) * (2.0 * math.pi / POS)
    turn_c, turn_s = jnp.cos(turn), jnp.sin(turn)
    turned = jnp.concatenate(
        [
            turn_c * spectra[:m] - turn_s * spectra[m:],
            turn_s * spectra[:m] + turn_c * spectra[m:],
        ],
        axis=0,
    )
    own = R_DEV * n
    place = (keys // (POS * R_DEV)) * own + owners * R_DEV + (keys // POS) % R_DEV
    spots = jnp.where(iota((SHELLS * own, keys.shape[1]), 0) == place, 1.0, 0.0).astype(BF16)
    summed = dot_nt(split(turned), spots)
    summed = (summed[: 2 * m] + summed[2 * m :]) * (1.0 / math.sqrt(NPHI))
    for j in range(m):
        send1[j, 0:1, :] = summed[j : j + 1]
        send1[j, 1:2, :] = summed[m + j : m + j + 1]

    def exchange(source, landing, send_sem, recv_sem):
        def post(step, carry):
            to = lax.rem(me + step, total)
            pltpu.make_async_remote_copy(
                src_ref=source(to), dst_ref=landing.at[me], send_sem=send_sem, recv_sem=recv_sem,
                device_id=(lax.rem(to, n), to // n), device_id_type=MESH,
            ).start()
            return carry

        lax.fori_loop(1, total, post, 0)
        pltpu.make_async_copy(source(me), landing.at[me], recv_sem).start()

    def drain(landing, sem, count):
        part = landing.at[pl.ds(0, count)]
        pltpu.make_async_copy(part, part, sem).wait()

    exchange(lambda to: send1.at[lax.rem(to, n)], recv1, s1_send, s1_recv)

    def second(t, carry):
        local[t] = partial(target_z(t) * INNER + my_y)
        return carry

    lax.fori_loop(0, depth, second, 0)

    width = table.shape[0]
    degree = (me_l * width + iota((1, width), 1)).astype(F32)
    smoothing = jnp.exp(-2.0 * degree * (degree + 1.0) / (degrees * degrees))
    factor = jnp.sqrt(
        jnp.maximum((degree - 1.0) * (degree + 2.0), 0.0) / jnp.maximum(degree * (degree + 1.0), 1.0)
    )
    shear = -0.5 * smoothing * factor
    for load in loads[1:]:
        load.wait()

    def forward(t):
        y_copy(t).wait_recv()
        send_z[t] = (local[t].astype(F32) + recv_y[t].astype(F32)).astype(BF16)
        z_copy(t).start()

    drain(recv1, s1_recv, total)
    line = iota((3 * GROUP, 1), 0)
    comp = line // GROUP
    part = (line // (SHELLS * R_DEV)) % 2
    shell = (line // R_DEV) % SHELLS
    from_sine = jnp.where(comp == 2, 1 - part, part) == 1
    sign = jnp.where((comp == 2) & (part == 1), -1.0, 1.0)
    blocks = []
    for q in range(nl):
        got = jnp.sum(recv1[q * n : (q + 1) * n], axis=0)
        cosine, sine = got[0:1], got[1:2]
        blocks.append(
            sign
            * jnp.where(
                from_sine,
                jnp.where(shell == 0, sine[:, :own], sine[:, own:]),
                jnp.where(shell == 0, cosine[:, :own], cosine[:, own:]),
            )
        )
    harmonics = jnp.concatenate(blocks, axis=1).astype(BF16)
    coefficients = dot_nt(harmonics, table[...])
    trace_terms = (coefficients[:GROUP] * smoothing).astype(BF16)
    shear_terms = (coefficients[GROUP:] * shear).astype(BF16)
    synthesis = jnp.concatenate(
        [
            jnp.dot(trace_terms, table[...], preferred_element_type=F32),
            jnp.dot(shear_terms[:GROUP], even[...], preferred_element_type=F32),
            jnp.dot(shear_terms[GROUP:], odd[...], preferred_element_type=F32),
            jnp.zeros((LANES - 3 * GROUP, table.shape[1]), F32),
        ],
        axis=0,
    )
    send2[...] = synthesis.T.reshape(total, R_DEV, LANES)
    exchange(lambda to: send2.at[to], recv2, s2_send, s2_recv)

    forward(0)

    for p in range(POS):
        turn = ((orders * p) % POS).astype(F32) * (2.0 * math.pi / POS)
        turn_c, turn_s = jnp.cos(turn), jnp.sin(turn)
        waves[:, p * SEG : (p + 1) * SEG] = split(
            jnp.concatenate(
                [turn_c * wave_c - turn_s * wave_s, turn_s * wave_c + turn_c * wave_s], axis=0
            )
        )

    if depth > 2:
        forward(1)

    drain(recv2, s2_recv, total)
    got = recv2[0:n]
    for q in range(1, nl):
        got = got + recv2[q * n : (q + 1) * n]
    own_line = iota(got.shape, 2) % R_DEV == iota(got.shape, 1)
    modes = jnp.sum(jnp.where(own_line, got, 0.0), axis=1).T
    halves = SHELLS * R_DEV
    sides = [
        jnp.concatenate(
            [modes[g * GROUP + c * halves : g * GROUP + (c + 1) * halves] for g in range(3)], axis=0
        )
        for c in range(2)
    ]
    stacked = jnp.concatenate(sides + sides, axis=1).astype(BF16)
    scale = 2.0 / math.sqrt(m)
    for p in range(POS):
        span = pl.ds(p * SEG, SEG)
        fields = jnp.dot(stacked, waves[:, span], preferred_element_type=F32) * scale
        half_trace = 0.5 * fields[:halves]
        first_part, second_part = fields[halves : 2 * halves], fields[2 * halves :]
        size = jnp.sqrt(first_part * first_part + second_part * second_part)
        for at, value in enumerate((half_trace + size, half_trace - size)):
            for s in range(SHELLS):
                eigen_ref[at, s, 0, :, span] = value[s * R_DEV : (s + 1) * R_DEV]

    def rest(t, carry):
        forward(t)
        return carry

    lax.fori_loop(min(2, depth - 1), depth - 1, rest, 0)

    y_copy(depth - 1).wait_recv()

    def landed(t, carry):
        z_copy(t).wait_recv()
        return carry

    lax.fori_loop(0, depth - 1, landed, 0)
    for p in range(POS):
        lines = pl.ds(p * halves, halves)

        def add(t, value):
            return value + recv_z[t, lines, :].astype(F32)

        value = local[depth - 1, lines, :].astype(F32) + recv_y[depth - 1, lines, :].astype(F32)
        value = lax.fori_loop(0, depth - 1, add, value)
        for s in range(SHELLS):
            cycle_ref[s, 0, :, pl.ds(p * SEG, SEG)] = value[s * R_DEV : (s + 1) * R_DEV]

    def sent_y(t, carry):
        y_copy(t).wait_send()
        return carry

    def sent_z(t, carry):
        z_copy(t).wait_send()
        return carry

    lax.fori_loop(0, depth, sent_y, 0)
    lax.fori_loop(0, depth - 1, sent_z, 0)
    drain(recv1, s1_send, total - 1)
    drain(recv2, s2_send, total - 1)


def body(partial_rows, row_owner, row_key, azimuth_orders, legendre_table, spin_even, spin_odd):
    n = lax.axis_size("blk")
    nl = lax.axis_size("lblk")
    total = n * nl
    depth = n // INNER
    count = partial_rows.shape[1]
    m = azimuth_orders.shape[0]
    width, cycles = legendre_table.shape[1:]
    block = (KEYS, SEG)
    vmem = pl.BlockSpec(memory_space=pltpu.VMEM)
    hbm = pl.BlockSpec(memory_space=pl.ANY)
    lanes = SHELLS * R_DEV * n
    dma = pltpu.SemaphoreType.DMA
    return pl.pallas_call(
        functools.partial(kernel, n, nl, float(width * nl)),
        out_shape=(
            jax.ShapeDtypeStruct((2, SHELLS, 1, R_DEV, NPHI), F32),
            jax.ShapeDtypeStruct((SHELLS, 1, R_DEV, NPHI), F32),
        ),
        in_specs=[hbm, vmem, vmem, vmem, hbm, hbm, hbm],
        out_specs=(vmem, vmem),
        scratch_shapes=[
            pltpu.VMEM((count, SEG), BF16),
            pltpu.VMEM((width, cycles), BF16),
            pltpu.VMEM((width, cycles), BF16),
            pltpu.VMEM((width, cycles), BF16),
            pltpu.VMEM((4 * m, NPHI), BF16),
            pltpu.VMEM((depth, *block), BF16),
            pltpu.VMEM((depth, *block), BF16),
            pltpu.VMEM((depth, *block), BF16),
            pltpu.VMEM((depth - 1, *block), BF16),
            pltpu.VMEM((depth - 1, *block), BF16),
            pltpu.VMEM((m, 2, lanes), F32),
            pltpu.VMEM((total, 2, lanes), F32),
            pltpu.VMEM((total, R_DEV, LANES), F32),
            pltpu.VMEM((total, R_DEV, LANES), F32),
            dma((4,)),
            dma((depth,)),
            dma((depth,)),
            dma((depth - 1,)),
            dma((depth - 1,)),
            dma,
            dma,
            dma,
            dma,
        ],
        compiler_params=pltpu.CompilerParams(
            collective_id=0, has_side_effects=True, vmem_limit_bytes=52 * 2**20
        ),
        cost_estimate=pl.CostEstimate(flops=6 * 10**9, bytes_accessed=6 * 10**6, transcendentals=10**5),
    )(
        partial_rows,
        row_owner.reshape(1, count),
        row_key,
        azimuth_orders.reshape(m, 1),
        legendre_table,
        spin_even,
        spin_odd,
    )


def solution(mesh):
    return jax.shard_map(
        body,
        mesh=mesh,
        in_specs=(
            P("lblk", "blk", None),
            P("lblk", "blk", None),
            P("lblk", "blk"),
            P(),
            P("blk", "lblk", None),
            P("blk", "lblk", None),
            P("blk", "lblk", None),
        ),
        out_specs=(P(None, None, "lblk", "blk", None), P(None, "lblk", "blk", None)),
        check_vma=False,
    )
```

```python
import functools
import math

import jax
import jax.numpy as jnp
from jax import lax
from jax.experimental import pallas as pl
from jax.experimental.pallas import tpu as pltpu
from jax.sharding import PartitionSpec as P

NPHI = 8192
SEG = 1024
R_DEV = 8
SHELLS = 2
POS = NPHI // SEG
KEYS = SHELLS * R_DEV * POS
LANES = 128
GROUP = 2 * SHELLS * R_DEV
INNER = 2
MESH = pl.DeviceIdType.MESH
F32 = jnp.float32
BF16 = jnp.bfloat16


def split(value):
    high = value.astype(BF16)
    low = (value - high.astype(F32)).astype(BF16)
    return jnp.concatenate([high, low], axis=0)


def dot_nt(a, b):
    return lax.dot_general(a, b, (((1,), (1,)), ((), ())), preferred_element_type=F32)


def iota(shape, axis):
    return lax.broadcasted_iota(jnp.int32, shape, axis)


def kernel(
    n, nl, degrees,
    rows_hbm, owner_hbm, key_hbm, order_hbm, table_hbm, even_hbm, odd_hbm,
    eigen_ref, cycle_ref,
    owner_ref, key_ref, order_ref, rows, table, even, odd, waves, send_y, local, recv_y, send_z, recv_z,
    send1, recv1, send2, recv2,
    load_sem, y_send, y_recv, z_send, z_recv, s1_send, s1_recv, s2_send, s2_recv,
):
    total = n * nl
    depth = n // INNER
    me_b = lax.axis_index("blk")
    me_l = lax.axis_index("lblk")
    me = me_l * n + me_b
    my_z = me_b // INNER
    my_y = me_b % INNER
    pair = my_z * INNER + (INNER - 1 - my_y)

    loads = [
        pltpu.make_async_copy(src, dst, load_sem.at[at])
        for at, (src, dst) in enumerate(
            ((order_hbm, order_ref), (key_hbm, key_ref), (owner_hbm, owner_ref), (rows_hbm.at[0], rows), (table_hbm.at[0], table), (even_hbm.at[0], even), (odd_hbm.at[0], odd))
        )
    ]
    for load in loads:
        load.start()

    barrier = pltpu.get_barrier_semaphore()

    def greet(step, carry):
        to = lax.rem(me + step, total)
        pl.semaphore_signal(barrier, inc=1, device_id=(lax.rem(to, n), to // n), device_id_type=MESH)
        return carry

    lax.fori_loop(1, total, greet, 0)

    for load in loads[:3]:
        load.wait()
    keys = key_ref[...]
    owners = owner_ref[...]
    slot = (keys % POS) * (SHELLS * R_DEV) + keys // POS
    m = order_ref.shape[1]
    spread = jnp.where(iota((m, m), 0) == iota((m, m), 1), order_ref[...].astype(F32), 0.0)
    orders = jnp.sum(spread, axis=1, keepdims=True).astype(jnp.int32)
    loads[3].wait()

    def partial(owner):
        chosen = jnp.where(owners == owner, slot, -1)
        one_hot = jnp.where(iota((KEYS, owners.shape[1]), 0) == chosen, 1.0, 0.0).astype(BF16)
        return jnp.dot(one_hot, rows[...], preferred_element_type=F32).astype(BF16)

    def target_z(t):
        return lax.rem(my_z + 1 + t, depth)

    def y_copy(t):
        return pltpu.make_async_remote_copy(
            src_ref=send_y.at[t], dst_ref=recv_y.at[t], send_sem=y_send.at[t], recv_sem=y_recv.at[t],
            device_id=(pair, me_l), device_id_type=MESH,
        )

    def z_copy(t):
        return pltpu.make_async_remote_copy(
            src_ref=send_z.at[t], dst_ref=recv_z.at[t], send_sem=z_send.at[t], recv_sem=z_recv.at[t],
            device_id=(target_z(t) * INNER + my_y, me_l), device_id_type=MESH,
        )

    def first(t, carry):
        send_y[t] = partial(target_z(t) * INNER + (INNER - 1 - my_y))
        y_copy(t).start()
        return carry

    pl.semaphore_wait(barrier, total - 1)
    lead, early = 0, min(1, depth)
    lax.fori_loop(0, lead, first, 0)
    phase = (iota((m, SEG), 1) * orders) % NPHI
    angle = phase.astype(F32) * (2.0 * math.pi / NPHI)
    wave_c, wave_s = jnp.cos(angle), jnp.sin(angle)
    eighth = ((iota((m, LANES), 1) * orders) % POS).astype(F32) * (2.0 * math.pi / POS)
    eighth_c, eighth_s = jnp.cos(eighth), jnp.sin(eighth)
    spectra = dot_nt(split(jnp.concatenate([wave_c, wave_s], axis=0)), rows[...])
    spectra = spectra[: 2 * m] + spectra[2 * m :]
    turn_c, turn_s = jnp.zeros((m, keys.shape[1]), F32), jnp.zeros((m, keys.shape[1]), F32)
    for p in range(POS):
        here = keys % POS == p
        turn_c = jnp.where(here, eighth_c[:, p : p + 1], turn_c)
        turn_s = jnp.where(here, eighth_s[:, p : p + 1], turn_s)
    turned = jnp.concatenate(
        [
            turn_c * spectra[:m] - turn_s * spectra[m:],
            turn_s * spectra[:m] + turn_c * spectra[m:],
        ],
        axis=0,
    )
    own = R_DEV * n
    place = (keys // (POS * R_DEV)) * own + owners * R_DEV + (keys // POS) % R_DEV
    spots = jnp.where(iota((SHELLS * own, keys.shape[1]), 0) == place, 1.0, 0.0).astype(BF16)
    summed = dot_nt(split(turned), spots)
    summed = (summed[: 2 * m] + summed[2 * m :]) * (1.0 / math.sqrt(NPHI))
    for j in range(m):
        send1[j, 0:1, :] = summed[j : j + 1]
        send1[j, 1:2, :] = summed[m + j : m + j + 1]

    def exchange(source, landing, send_sem, recv_sem):
        def post(step, carry):
            to = lax.rem(me + step, total)
            pltpu.make_async_remote_copy(
                src_ref=source(to), dst_ref=landing.at[me], send_sem=send_sem, recv_sem=recv_sem,
                device_id=(lax.rem(to, n), to // n), device_id_type=MESH,
            ).start()
            return carry

        lax.fori_loop(1, total, post, 0)
        pltpu.make_async_copy(source(me), landing.at[me], recv_sem).start()

    def drain(landing, sem, count):
        part = landing.at[pl.ds(0, count)]
        pltpu.make_async_copy(part, part, sem).wait()

    exchange(lambda to: send1.at[lax.rem(to, n)], recv1, s1_send, s1_recv)
    lax.fori_loop(lead, early, first, 0)

    def second(t, carry):
        local[t] = partial(target_z(t) * INNER + my_y)
        return carry

    lax.fori_loop(0, depth, second, 0)

    width = table.shape[0]
    degree = (me_l * width + iota((1, width), 1)).astype(F32)
    smoothing = jnp.exp(-2.0 * degree * (degree + 1.0) / (degrees * degrees))
    factor = jnp.sqrt(
        jnp.maximum((degree - 1.0) * (degree + 2.0), 0.0) / jnp.maximum(degree * (degree + 1.0), 1.0)
    )
    shear = -0.5 * smoothing * factor
    for load in loads[4:]:
        load.wait()

    def forward(t):
        y_copy(t).wait_recv()
        send_z[t] = (local[t].astype(F32) + recv_y[t].astype(F32)).astype(BF16)
        z_copy(t).start()

    drain(recv1, s1_recv, total)
    line = iota((3 * GROUP, 1), 0)
    comp = line // GROUP
    part = (line // (SHELLS * R_DEV)) % 2
    shell = (line // R_DEV) % SHELLS
    from_sine = jnp.where(comp == 2, 1 - part, part) == 1
    sign = jnp.where((comp == 2) & (part == 1), -1.0, 1.0)
    blocks = []
    for q in range(nl):
        got = jnp.sum(recv1[q * n : (q + 1) * n], axis=0)
        cosine, sine = got[0:1], got[1:2]
        blocks.append(
            sign
            * jnp.where(
                from_sine,
                jnp.where(shell == 0, sine[:, :own], sine[:, own:]),
                jnp.where(shell == 0, cosine[:, :own], cosine[:, own:]),
            )
        )
    harmonics = jnp.concatenate(blocks, axis=1).astype(BF16)
    coefficients = dot_nt(harmonics, table[...])
    trace_terms = (coefficients[:GROUP] * smoothing).astype(BF16)
    shear_terms = (coefficients[GROUP:] * shear).astype(BF16)
    synthesis = jnp.concatenate(
        [
            jnp.dot(trace_terms, table[...], preferred_element_type=F32),
            jnp.dot(shear_terms[:GROUP], even[...], preferred_element_type=F32),
            jnp.dot(shear_terms[GROUP:], odd[...], preferred_element_type=F32),
            jnp.zeros((LANES - 3 * GROUP, table.shape[1]), F32),
        ],
        axis=0,
    )
    send2[...] = synthesis.T.reshape(total, R_DEV, LANES)
    exchange(lambda to: send2.at[to], recv2, s2_send, s2_recv)
    lax.fori_loop(early, depth, first, 0)

    forward(0)

    for p in range(POS):
        turn_c, turn_s = eighth_c[:, p : p + 1], eighth_s[:, p : p + 1]
        waves[:, p * SEG : (p + 1) * SEG] = split(
            jnp.concatenate(
                [turn_c * wave_c - turn_s * wave_s, turn_s * wave_c + turn_c * wave_s], axis=0
            )
        )

    def rest(t, carry):
        forward(t)
        return carry

    lax.fori_loop(1, depth - 1, rest, 0)
    drain(recv2, s2_recv, total)
    got = recv2[0:n]
    for q in range(1, nl):
        got = got + recv2[q * n : (q + 1) * n]
    own_line = iota(got.shape, 2) % R_DEV == iota(got.shape, 1)
    modes = jnp.sum(jnp.where(own_line, got, 0.0), axis=1).T
    halves = SHELLS * R_DEV
    sides = [
        jnp.concatenate(
            [modes[g * GROUP + c * halves : g * GROUP + (c + 1) * halves] for g in range(3)], axis=0
        )
        for c in range(2)
    ]
    stacked = jnp.concatenate(sides + sides, axis=1).astype(BF16)
    scale = 2.0 / math.sqrt(m)
    for p in range(POS):
        span = pl.ds(p * SEG, SEG)
        fields = jnp.dot(stacked, waves[:, span], preferred_element_type=F32) * scale
        half_trace = 0.5 * fields[:halves]
        first_part, second_part = fields[halves : 2 * halves], fields[2 * halves :]
        size = jnp.sqrt(first_part * first_part + second_part * second_part)
        for at, value in enumerate((half_trace + size, half_trace - size)):
            for s in range(SHELLS):
                eigen_ref[at, s, 0, :, span] = value[s * R_DEV : (s + 1) * R_DEV]

    y_copy(depth - 1).wait_recv()

    def landed(t, carry):
        z_copy(t).wait_recv()
        return carry

    lax.fori_loop(0, depth - 1, landed, 0)
    for p in range(POS):
        lines = pl.ds(p * halves, halves)

        def add(t, value):
            return value + recv_z[t, lines, :].astype(F32)

        value = local[depth - 1, lines, :].astype(F32) + recv_y[depth - 1, lines, :].astype(F32)
        value = lax.fori_loop(0, depth - 1, add, value)
        for s in range(SHELLS):
            cycle_ref[s, 0, :, pl.ds(p * SEG, SEG)] = value[s * R_DEV : (s + 1) * R_DEV]

    def sent_y(t, carry):
        y_copy(t).wait_send()
        return carry

    def sent_z(t, carry):
        z_copy(t).wait_send()
        return carry

    lax.fori_loop(0, depth, sent_y, 0)
    lax.fori_loop(0, depth - 1, sent_z, 0)
    drain(recv1, s1_send, total - 1)
    drain(recv2, s2_send, total - 1)


def body(partial_rows, row_owner, row_key, azimuth_orders, legendre_table, spin_even, spin_odd):
    n = lax.axis_size("blk")
    nl = lax.axis_size("lblk")
    total = n * nl
    depth = n // INNER
    count = partial_rows.shape[1]
    m = azimuth_orders.shape[0]
    width, cycles = legendre_table.shape[1:]
    block = (KEYS, SEG)
    vmem = pl.BlockSpec(memory_space=pltpu.VMEM)
    hbm = pl.BlockSpec(memory_space=pltpu.HBM)
    lanes = SHELLS * R_DEV * n
    dma = pltpu.SemaphoreType.DMA
    return pl.pallas_call(
        functools.partial(kernel, n, nl, float(width * nl)),
        out_shape=(
            jax.ShapeDtypeStruct((2, SHELLS, 1, R_DEV, NPHI), F32),
            jax.ShapeDtypeStruct((SHELLS, 1, R_DEV, NPHI), F32),
        ),
        in_specs=[hbm] * 7,
        out_specs=(vmem, vmem),
        scratch_shapes=[
            pltpu.VMEM((1, count), jnp.int32),
            pltpu.VMEM((1, count), jnp.int32),
            pltpu.VMEM((1, m), jnp.int32),
            pltpu.VMEM((count, SEG), BF16),
            pltpu.VMEM((width, cycles), BF16),
            pltpu.VMEM((width, cycles), BF16),
            pltpu.VMEM((width, cycles), BF16),
            pltpu.VMEM((4 * m, NPHI), BF16),
            pltpu.VMEM((depth, *block), BF16),
            pltpu.VMEM((depth, *block), BF16),
            pltpu.VMEM((depth, *block), BF16),
            pltpu.VMEM((depth - 1, *block), BF16),
            pltpu.VMEM((depth - 1, *block), BF16),
            pltpu.VMEM((m, 2, lanes), F32),
            pltpu.VMEM((total, 2, lanes), F32),
            pltpu.VMEM((total, R_DEV, LANES), F32),
            pltpu.VMEM((total, R_DEV, LANES), F32),
            dma((7,)),
            dma((depth,)),
            dma((depth,)),
            dma((depth - 1,)),
            dma((depth - 1,)),
            dma,
            dma,
            dma,
            dma,
        ],
        compiler_params=pltpu.CompilerParams(
            collective_id=0, has_side_effects=True, vmem_limit_bytes=62 * 2**20
        ),
        cost_estimate=pl.CostEstimate(flops=6 * 10**9, bytes_accessed=6 * 10**6, transcendentals=10**5),
    )(
        partial_rows,
        row_owner.reshape(1, count),
        row_key,
        azimuth_orders.reshape(1, m),
        legendre_table,
        spin_even,
        spin_odd,
    )


def solution(mesh):
    return jax.shard_map(
        body,
        mesh=mesh,
        in_specs=(
            P("lblk", "blk", None),
            P("lblk", "blk", None),
            P("lblk", "blk"),
            P(),
            P("blk", "lblk", None),
            P("blk", "lblk", None),
            P("blk", "lblk", None),
        ),
        out_specs=(P(None, None, "lblk", "blk", None), P(None, "lblk", "blk", None)),
        check_vma=False,
    )
```
